256 devices in a mesh: row: 8 (over x, core), col: 8 (over z), layer: 4 (over y).
Axes of the slice: x: 4, y: 4, z: 8, core: 2. Of those that a mesh axis runs over, the one named last changes fastest.
Arguments:
- amplitudes: float32 [512, 147456], P('col', ('row', 'layer')), may hold values from -6 to 6
- integrals: float32 [1024, 147456], P('col', ('row', 'layer')), may hold values from -0.015625 to 0.015625
Outputs:
- ladder: float32 [512, 1024], P(('row', 'layer'), 'col')
The draws below stay inside these ranges and needn't reach their ends.
All inputs are finite; a program needn't handle non-finite values.
Results may differ from the reference program's by a relative error of at most 0.000082.
Values sent between devices are 32-bit elements; how exact they have to be, the bound alone decides.
No kernel may reach another device: no remote copies, remote signals or barrier semaphores. Data moves between devices by JAX's collectives and lax.ppermute only.
A program may use at most 64 MiB of HBM per device.

```python
import jax
import jax.numpy as jnp
from jax import lax

IJ = 512
AB = 1024
CD = 147456


def spiked(array, key, source, target, parts, factor):
    owner, partner = [(jnp.arange(array.shape[position]) // (array.shape[position] // parts)).reshape([-1 if axis == position else 1 for axis in range(array.ndim)]) for position in (source, target)]
    chosen = jax.random.permutation(key, parts)[partner]
    strong = (owner == chosen) | (owner == (partner + parts // 2) % parts)
    return jnp.where(strong, factor * array, array)


def block_scale(stream_key, extent, pieces, low, high):
    def one(dim, parts):
        draws = jax.random.uniform(jax.random.fold_in(jax.random.fold_in(stream_key, 6), dim), (parts,), jnp.float32, low / len(pieces), high / len(pieces))
        return jnp.repeat(jnp.exp(draws), extent[dim] // parts).reshape((-1,) + (1,) * (len(extent) - dim - 1))

    factor_of = one(*pieces[0])
    for cut in pieces[1:]:
        factor_of = factor_of * one(*cut)
    return factor_of


def scatter_about(key, dims, spread, bound, cuts=(), kind=jnp.bfloat16):
    loudness = block_scale(key, dims, cuts, -0.22, 0.18) if cuts else 1.0
    values = jax.random.normal(key, dims, jnp.float32) * spread * loudness
    return jnp.minimum(jnp.maximum(values, -bound), bound).astype(kind)


def heavy_noise(own_key, shape, deviation, most, split, heavy, held_as=jnp.bfloat16):
    values = deviation * jax.random.normal(own_key, shape, jnp.float32)
    if split:
        values = values * block_scale(own_key, shape, split, -0.22, 0.18)
    return jnp.clip(spiked(values, jax.random.fold_in(own_key, 3), *heavy), -most, most).astype(held_as)


def setup_inputs(seed: int = 0) -> dict:
    key_list = jax.random.split(jax.random.key(seed), 3)
    return {
        "amplitudes": heavy_noise(key_list[0], (IJ, CD), 1.0, 6.0, ((0, 8), (1, 32)), (1, 0, 32, 2.75), jnp.float32),
        "integrals": scatter_about(key_list[1], (AB, CD), CD ** -0.5, 0.015625, ((0, 8), (1, 32)), jnp.float32),
    }


def reference(amplitudes, integrals):
    contraction = lax.dot_general(amplitudes, integrals, (((1,), (1,)), ((), ())), precision=lax.Precision.HIGHEST, preferred_element_type=jnp.float32)
    return 0.5 * contraction
```

```python
import jax
import jax.numpy as jnp
from jax import lax
from jax.sharding import PartitionSpec as P


def contract_last(left, right):
    return lax.dot_general(
        left,
        right,
        (((1,), (1,)), ((), ())),
        precision=lax.Precision.HIGHEST,
        preferred_element_type=jnp.float32,
    )


def on_device(amplitudes, integrals):
    partial_sum = contract_last(lax.all_gather(amplitudes, "col", axis=0, tiled=True), integrals)
    rows, columns = partial_sum.shape
    shares = lax.axis_size(("row", "layer"))
    blocks = (0.5 * partial_sum).reshape(shares, rows // shares, columns)
    return lax.all_to_all(blocks, ("row", "layer"), 0, 0).sum(0)


def solution(mesh):
    in_specs = (P("col", ("row", "layer")), P("col", ("row", "layer")))
    out_specs = P(("row", "layer"), "col")
    return jax.shard_map(
        on_device, mesh=mesh, in_specs=in_specs, out_specs=out_specs, check_vma=False
    )
```

```python
import jax
import jax.numpy as jnp
from jax import lax
from jax.sharding import PartitionSpec as P


def contract_last(left, right):
    return lax.dot_general(
        left,
        right,
        (((1,), (1,)), ((), ())),
        precision=lax.Precision.HIGHEST,
        preferred_element_type=jnp.float32,
    )


def on_device(amplitudes, integrals):
    levels = lax.axis_size("col")
    half = amplitudes.shape[1] // 2
    far = levels // 2
    a_parts = [amplitudes[:, :half], amplitudes[:, half:]]
    b_parts = [integrals[:, :half], integrals[:, half:]]
    hop_up = [(i, (i + 1) % levels) for i in range(levels)]
    hop_down = [(i, (i - 1) % levels) for i in range(levels)]

    terms = [[] for _ in range(levels)]
    terms[0] = [contract_last(a, b) for a, b in zip(a_parts, b_parts)]
    up, down = list(a_parts), list(a_parts)
    for hop in range(1, far):
        for i in (0, 1):
            up[i] = lax.ppermute(up[i], "col", hop_up)
            down[1 - i] = lax.ppermute(down[1 - i], "col", hop_down)
        for i in (0, 1):
            terms[-hop % levels].append(contract_last(up[i], b_parts[i]))
            terms[hop].append(contract_last(down[1 - i], b_parts[1 - i]))
    terms[far].append(contract_last(lax.ppermute(up[0], "col", hop_up), b_parts[0]))
    terms[far].append(contract_last(lax.ppermute(down[1], "col", hop_down), b_parts[1]))

    by_distance = jnp.stack([0.5 * (t[0] + t[1]) for t in terms])
    partial_sum = jnp.roll(by_distance, lax.axis_index("col"), axis=0)
    shares = lax.axis_size(("row", "layer"))
    blocks = partial_sum.reshape(shares, -1, partial_sum.shape[-1])
    return lax.all_to_all(blocks, ("row", "layer"), 0, 0).sum(0)


def solution(mesh):
    in_specs = (P("col", ("row", "layer")), P("col", ("row", "layer")))
    out_specs = P(("row", "layer"), "col")
    return jax.shard_map(
        on_device, mesh=mesh, in_specs=in_specs, out_specs=out_specs, check_vma=False
    )
```

```python
import jax
import jax.numpy as jnp
from jax import lax
from jax.experimental import pallas as pl
from jax.experimental.pallas import tpu as pltpu
from jax.sharding import PartitionSpec as P


def multiply(blocks, places, b, before):
    count = len(blocks)
    height = blocks[0].shape[0]
    levels = before.shape[0]

    def kernel(*refs):
        b_ref, old, out = refs[count:]
        level = lax.axis_index("col")
        out[...] = old[...]
        left = jnp.concatenate([ref[...] for ref in refs[:count]], axis=0)
        product = 0.5 * lax.dot_general(
            left,
            b_ref[...],
            (((1,), (1,)), ((), ())),
            precision=lax.Precision.HIGHEST,
            preferred_element_type=jnp.float32,
        )
        for i, (distance, half) in enumerate(places):
            index = lax.rem(level + distance % levels, levels)
            out[index, half * height : (half + 1) * height] = product[i * height : (i + 1) * height]

    return pl.pallas_call(
        kernel,
        out_shape=jax.ShapeDtypeStruct(before.shape, jnp.float32),
        in_specs=[pl.BlockSpec(memory_space=pltpu.VMEM)] * (count + 2),
        out_specs=pl.BlockSpec(memory_space=pltpu.VMEM),
        input_output_aliases={count + 1: 0},
        compiler_params=pltpu.CompilerParams(vmem_limit_bytes=32 * 1024 * 1024),
    )(*blocks, b, before)


def on_device(amplitudes, integrals):
    levels = lax.axis_size("col")
    rows, columns = amplitudes.shape[0], integrals.shape[0]
    height = rows // 2
    hop_up = [(i, (i + 1) % levels) for i in range(levels)]
    hop_down = [(i, (i - 1) % levels) for i in range(levels)]

    first = amplitudes[:height]
    later, first = lax.optimization_barrier((amplitudes, first))
    second = later[height:]

    product = jnp.zeros((levels, rows, columns), jnp.float32)
    up, down = [first, second], [first, second]
    product = multiply([first, second], [(0, 0), (0, 1)], integrals, product)
    for hop in range(1, levels // 2):
        for i in (0, 1):
            up[i] = lax.ppermute(up[i], "col", hop_up)
            down[1 - i] = lax.ppermute(down[1 - i], "col", hop_down)
            product = multiply([up[i], down[1 - i]], [(-hop, i), (hop, 1 - i)], integrals, product)
    up_half = lax.ppermute(up[0], "col", hop_up)
    down_half = lax.ppermute(down[1], "col", hop_down)
    far = levels // 2
    product = multiply([up_half, down_half], [(far, 0), (far, 1)], integrals, product)

    shares = lax.axis_size(("row", "layer"))
    blocks = product.reshape(shares, -1, columns)
    return lax.all_to_all(blocks, ("row", "layer"), 0, 0).sum(0)


def solution(mesh):
    in_specs = (P("col", ("row", "layer")), P("col", ("row", "layer")))
    out_specs = P(("row", "layer"), "col")
    return jax.shard_map(
        on_device, mesh=mesh, in_specs=in_specs, out_specs=out_specs, check_vma=False
    )
```

```python
import jax
import jax.numpy as jnp
from jax import lax
from jax.experimental import pallas as pl
from jax.experimental.pallas import tpu as pltpu
from jax.sharding import PartitionSpec as P

def transposed(array):
    def kernel(src, out):
        out[...] = src[...].T

    return pl.pallas_call(
        kernel,
        out_shape=jax.ShapeDtypeStruct(array.shape[::-1], array.dtype),
        in_specs=[pl.BlockSpec(memory_space=pltpu.VMEM)],
        out_specs=pl.BlockSpec(memory_space=pltpu.VMEM),
        compiler_params=pltpu.CompilerParams(vmem_limit_bytes=32 * 1024 * 1024),
    )(array)


def multiply(blocks, places, b, before):
    count = len(blocks)
    height = blocks[0].shape[0]
    levels = before.shape[0]

    def kernel(*refs):
        b_ref, old, out = refs[count:]
        level = lax.axis_index("col")
        out[...] = old[...]
        left = jnp.concatenate([ref[...] for ref in refs[:count]], axis=0)
        product = 0.5 * jnp.dot(
            left,
            b_ref[...],
            precision=lax.Precision.HIGHEST,
            preferred_element_type=jnp.float32,
        )
        for i, (distance, half) in enumerate(places):
            index = lax.rem(level + distance % levels, levels)
            out[index, half * height : (half + 1) * height] = product[i * height : (i + 1) * height]

    return pl.pallas_call(
        kernel,
        out_shape=jax.ShapeDtypeStruct(before.shape, jnp.float32),
        in_specs=[pl.BlockSpec(memory_space=pltpu.VMEM)] * (count + 2),
        out_specs=pl.BlockSpec(memory_space=pltpu.VMEM),
        input_output_aliases={count + 1: 0},
        compiler_params=pltpu.CompilerParams(vmem_limit_bytes=32 * 1024 * 1024),
    )(*blocks, b, before)


def on_device(amplitudes, integrals):
    levels = lax.axis_size("col")
    rows, columns = amplitudes.shape[0], integrals.shape[0]
    hop_up = [(i, (i + 1) % levels) for i in range(levels)]
    hop_down = [(i, (i - 1) % levels) for i in range(levels)]

    height = rows // 2
    first, second = lax.optimization_barrier((amplitudes[:height], amplitudes[height:]))
    b = transposed(integrals)

    product = jnp.zeros((levels, rows, columns), jnp.float32)
    up, down = [first, second], [first, second]
    product = multiply([first, second], [(0, 0), (0, 1)], b, product)
    for hop in range(1, levels // 2):
        for i in (0, 1):
            up[i] = lax.ppermute(up[i], "col", hop_up)
            down[1 - i] = lax.ppermute(down[1 - i], "col", hop_down)
            product = multiply([up[i], down[1 - i]], [(-hop, i), (hop, 1 - i)], b, product)
    up_half = lax.ppermute(up[0], "col", hop_up)
    down_half = lax.ppermute(down[1], "col", hop_down)
    far = levels // 2
    product = multiply([up_half, down_half], [(far, 0), (far, 1)], b, product)

    shares = lax.axis_size(("row", "layer"))
    blocks = product.reshape(shares, -1, columns)
    return lax.all_to_all(blocks, ("row", "layer"), 0, 0).sum(0)


def solution(mesh):
    in_specs = (P("col", ("row", "layer")), P("col", ("row", "layer")))
    out_specs = P(("row", "layer"), "col")
    return jax.shard_map(
        on_device, mesh=mesh, in_specs=in_specs, out_specs=out_specs, check_vma=False
    )
```

```python
import jax
import jax.numpy as jnp
from jax import lax
from jax.experimental import pallas as pl
from jax.experimental.pallas import tpu as pltpu
from jax.sharding import Mesh
from jax.sharding import PartitionSpec as P

LEVELS = 8
EARLY = 48
COL = ("zhi", "zlo")
VMEM = pl.BlockSpec(memory_space=pltpu.VMEM)
SWAP_1 = [(i, i ^ 1) for i in range(LEVELS)]
SWAP_2 = [((i + 1) % LEVELS, (j + 1) % LEVELS) for i, j in SWAP_1]


def swap_1(array):
    return lax.ppermute(array, COL, SWAP_1)


def swap_2(array):
    return lax.ppermute(array, COL, SWAP_2)


def after(done, *payloads):
    return lax.optimization_barrier((*payloads, *done))[: len(payloads)]


def dot(left, right):
    return 0.5 * jnp.dot(
        left, right, precision=lax.Precision.HIGHEST, preferred_element_type=jnp.float32
    )


def transposed(array):
    def kernel(src, out):
        out[...] = src[...].T

    return pl.pallas_call(
        kernel,
        out_shape=jax.ShapeDtypeStruct(array.shape[::-1], array.dtype),
        in_specs=[VMEM],
        out_specs=VMEM,
        compiler_params=pltpu.CompilerParams(vmem_limit_bytes=16 * 1024 * 1024),
    )(array)


def row_level(level, distance):
    away = jnp.where(lax.rem(level, 2) == 0, distance % LEVELS, -distance % LEVELS)
    return lax.rem(level + away, LEVELS)


def multiply(blocks, distances, b, before):
    count = len(blocks)

    def kernel(*refs):
        b_ref, old, out = refs[count:]
        level = lax.axis_index("zhi") * 2 + lax.axis_index("zlo")
        out[...] = old[...]
        for ref, distance in zip(refs, distances):
            out[lax.axis_index("zlo"), row_level(level, distance)] = dot(ref[...], b_ref[...])

    return pl.pallas_call(
        kernel,
        out_shape=jax.ShapeDtypeStruct(before.shape, jnp.float32),
        in_specs=[VMEM] * (count + 2),
        out_specs=VMEM,
        input_output_aliases={count + 1: 0},
        compiler_params=pltpu.CompilerParams(vmem_limit_bytes=24 * 1024 * 1024),
    )(*blocks, b, before)


def split(array):
    high = array.astype(jnp.bfloat16)
    return high, (array - high.astype(jnp.float32)).astype(jnp.bfloat16)


def split_stack(blocks):
    count, (rows, width) = len(blocks), blocks[0].shape

    def kernel(*refs):
        high, low = refs[count:]
        for i, ref in enumerate(refs[:count]):
            place = slice(i * rows, (i + 1) * rows)
            high[place, :], low[place, :] = split(ref[...])

    return pl.pallas_call(
        kernel,
        out_shape=[jax.ShapeDtypeStruct((count * rows, width), jnp.bfloat16)] * 2,
        in_specs=[VMEM] * count,
        out_specs=[VMEM] * 2,
        compiler_params=pltpu.CompilerParams(vmem_limit_bytes=24 * 1024 * 1024),
    )(*blocks)


def finish(last, b, before, stack, distances, pair_b):
    rows = last.shape[0]

    def kernel(last_ref, b_ref, high, low, *refs):
        pair_refs, old, out = refs[:-2], refs[-2], refs[-1]
        odd = lax.axis_index("zlo")
        level = lax.axis_index("zhi") * 2 + odd
        out[...] = old[...]
        block = last_ref[...]
        out[odd, row_level(level, LEVELS // 2)] = dot(block, b_ref[...])
        b_high, b_low = split(jnp.concatenate([ref[...] for ref in pair_refs], axis=0).T)

        def product(a_high, a_low):
            terms = [(a_low, b_high), (a_high, b_low), (a_high, b_high)]
            return 0.5 * sum(jnp.dot(*t, preferred_element_type=jnp.float32) for t in terms)

        early = product(high[...], low[...])
        for i, distance in enumerate(distances):
            out[1 - odd, row_level(level, distance)] = early[i * rows : (i + 1) * rows]
        out[1 - odd, row_level(level, LEVELS // 2)] = product(*split(block))

    return pl.pallas_call(
        kernel,
        out_shape=jax.ShapeDtypeStruct(before.shape, jnp.float32),
        in_specs=[VMEM] * (5 + len(pair_b)),
        out_specs=VMEM,
        input_output_aliases={4 + len(pair_b): 0},
        compiler_params=pltpu.CompilerParams(vmem_limit_bytes=24 * 1024 * 1024),
    )(last, b, *stack, *pair_b, before)


def on_device(amplitudes, integrals):
    level = lax.axis_index("zhi") * 2 + lax.axis_index("zlo")
    held = (level + 1) // 2 % 2
    rows, columns = amplitudes.shape[0], integrals.shape[0]
    half = amplitudes.shape[1] // 2

    def halves(array):
        low, high = array[:, :half], array[:, half:]
        return jnp.where(held == 0, low, high), jnp.where(held == 0, high, low)

    a_own, a_other = lax.optimization_barrier(halves(amplitudes))
    b_own, b_other = halves(integrals)

    far_1, far_2 = swap_1(a_own), swap_2(a_other)
    a_1, a_2 = swap_1(a_other), swap_2(a_own)
    a_3, far_2 = swap_1(far_2), swap_2(far_1)
    b_early, a_1_on = after((a_1, a_2), b_other[:EARLY], a_1)
    pair_early, a_4 = swap_1(b_early), swap_2(a_1_on)
    a_5, a_6 = swap_1(far_2), swap_2(a_3)
    (b_late,) = after((pair_early, a_4), b_other[EARLY:])
    a_7, pair_late = swap_2(a_5), swap_1(b_late)

    b = transposed(b_own)
    product = jnp.zeros((2, LEVELS, rows, columns), jnp.float32)
    early, distances = [a_own, a_1, a_2, a_3, a_4, a_6, a_5], [0, 1, -1, 2, -2, -3, 3]
    for part in (slice(0, 3), slice(3, 5), slice(5, 7)):
        product = multiply(early[part], distances[part], b, product)
    pair_b = [pair_early, pair_late]
    product = finish(a_7, b, product, split_stack(early), distances, pair_b)

    axes = ("zlo", "row", "layer")
    blocks = product.reshape(lax.axis_size(axes), -1, columns)
    return lax.all_to_all(blocks, axes, 0, 0).sum(0)


def solution(mesh):
    rows, _, layers = mesh.devices.shape
    fine = Mesh(mesh.devices.reshape(rows, -1, 2, layers), ("row", "zhi", "zlo", "layer"))
    split = ("row", "layer")
    return jax.shard_map(
        on_device,
        mesh=fine,
        in_specs=(P(COL, split), P(COL, split)),
        out_specs=P(split, COL),
        check_vma=False,
    )
```

```python
import jax
import jax.numpy as jnp
from jax import lax
from jax.experimental import pallas as pl
from jax.experimental.pallas import tpu as pltpu
from jax.sharding import Mesh
from jax.sharding import PartitionSpec as P

LEVELS = 8
EARLY = 48
COL = ("zhi", "zlo")
VMEM = pl.BlockSpec(memory_space=pltpu.VMEM)
SWAP_1 = [(i, i ^ 1) for i in range(LEVELS)]
SWAP_2 = [((i + 1) % LEVELS, (j + 1) % LEVELS) for i, j in SWAP_1]


def swap_1(array):
    return lax.ppermute(array, COL, SWAP_1)


def swap_2(array):
    return lax.ppermute(array, COL, SWAP_2)


def after(done, *payloads):
    return lax.optimization_barrier((*payloads, *done))[: len(payloads)]


def dot(left, right):
    return 0.5 * jnp.dot(
        left, right, precision=lax.Precision.HIGHEST, preferred_element_type=jnp.float32
    )


def transposed(array):
    def kernel(src, out):
        out[...] = src[...].T

    return pl.pallas_call(
        kernel,
        out_shape=jax.ShapeDtypeStruct(array.shape[::-1], array.dtype),
        in_specs=[VMEM],
        out_specs=VMEM,
        compiler_params=pltpu.CompilerParams(vmem_limit_bytes=16 * 1024 * 1024),
    )(array)


def row_level(level, distance):
    away = jnp.where(lax.rem(level, 2) == 0, distance % LEVELS, -distance % LEVELS)
    return lax.rem(level + away, LEVELS)


def multiply(blocks, distances, b, before):
    count = len(blocks)

    def kernel(*refs):
        b_ref, old, out = refs[count:]
        level = lax.axis_index("zhi") * 2 + lax.axis_index("zlo")
        out[...] = old[...]
        for ref, distance in zip(refs, distances):
            source = row_level(level, distance)
            out[lax.rem(source, 2), lax.axis_index("zlo"), source // 2] = dot(ref[...], b_ref[...])

    return pl.pallas_call(
        kernel,
        out_shape=jax.ShapeDtypeStruct(before.shape, jnp.float32),
        in_specs=[VMEM] * (count + 2),
        out_specs=VMEM,
        input_output_aliases={count + 1: 0},
        compiler_params=pltpu.CompilerParams(vmem_limit_bytes=24 * 1024 * 1024),
    )(*blocks, b, before)


def split(array):
    high = array.astype(jnp.bfloat16)
    return high, (array - high.astype(jnp.float32)).astype(jnp.bfloat16)


def split_stack(blocks):
    count, (rows, width) = len(blocks), blocks[0].shape

    def kernel(*refs):
        high, low = refs[count:]
        for i, ref in enumerate(refs[:count]):
            place = slice(i * rows, (i + 1) * rows)
            high[place, :], low[place, :] = split(ref[...])

    return pl.pallas_call(
        kernel,
        out_shape=[jax.ShapeDtypeStruct((count * rows, width), jnp.bfloat16)] * 2,
        in_specs=[VMEM] * count,
        out_specs=[VMEM] * 2,
        compiler_params=pltpu.CompilerParams(vmem_limit_bytes=24 * 1024 * 1024),
    )(*blocks)


def finish(last, b, before, stack, distances, pair_b):
    rows = last.shape[0]

    def kernel(last_ref, b_ref, high, low, *refs):
        pair_refs, old, mine, other = refs[:-3], refs[-3], refs[-2], refs[-1]
        core, odd = lax.axis_index("core"), lax.axis_index("zlo")
        level = lax.axis_index("zhi") * 2 + odd
        mine[odd] = old[core, odd]
        other[odd] = old[1 - core, odd]

        def store(column, distance, product):
            source = row_level(level, distance)

            @pl.when(lax.rem(source, 2) == core)
            def _():
                mine[column, source // 2] = product

            @pl.when(lax.rem(source, 2) != core)
            def _():
                other[column, source // 2] = product

        block = last_ref[...]
        store(odd, LEVELS // 2, dot(block, b_ref[...]))
        b_high, b_low = split(jnp.concatenate([ref[...] for ref in pair_refs], axis=0).T)

        def product(a_high, a_low):
            terms = [(a_low, b_high), (a_high, b_low), (a_high, b_high)]
            return 0.5 * sum(jnp.dot(*t, preferred_element_type=jnp.float32) for t in terms)

        early = product(high[...], low[...])
        for i, distance in enumerate(distances):
            store(1 - odd, distance, early[i * rows : (i + 1) * rows])
        store(1 - odd, LEVELS // 2, product(*split(block)))

    return pl.pallas_call(
        kernel,
        out_shape=[jax.ShapeDtypeStruct(before.shape[1:], jnp.float32)] * 2,
        in_specs=[VMEM] * (5 + len(pair_b)),
        out_specs=[VMEM] * 2,
        compiler_params=pltpu.CompilerParams(vmem_limit_bytes=24 * 1024 * 1024),
    )(last, b, *stack, *pair_b, before)


def on_device(amplitudes, integrals):
    level = lax.axis_index("zhi") * 2 + lax.axis_index("zlo")
    held = (level + 1) // 2 % 2
    rows, columns = amplitudes.shape[0], integrals.shape[0]
    half = amplitudes.shape[1] // 2

    def halves(array):
        low, high = array[:, :half], array[:, half:]
        return jnp.where(held == 0, low, high), jnp.where(held == 0, high, low)

    a_own, a_other = lax.optimization_barrier(halves(amplitudes))
    b_own, b_other = halves(integrals)

    far_1, far_2 = swap_1(a_own), swap_2(a_other)
    a_1, a_2 = swap_1(a_other), swap_2(a_own)
    a_3, far_3 = swap_1(far_2), swap_2(far_1)
    b_early, a_1_on = after((a_1, a_2), b_other[:EARLY], a_1)
    pair_early, a_4 = swap_1(b_early), swap_2(a_1_on)
    a_5, a_6 = swap_1(far_3), swap_2(a_3)
    (b_late,) = after((pair_early, a_4), b_other[EARLY:])
    a_7, pair_late = swap_2(a_5), swap_1(b_late)

    b = transposed(b_own)
    product = jnp.zeros((2, 2, LEVELS // 2, rows, columns), jnp.float32)
    early, distances = [a_own, a_1, a_2, a_3, a_4, a_6, a_5], [0, 1, -1, 2, -2, -3, 3]
    for part in (slice(0, 3), slice(3, 5), slice(5, 7)):
        product = multiply(early[part], distances[part], b, product)
    pair_b = [pair_early, pair_late]
    mine, other = finish(a_7, b, product, split_stack(early), distances, pair_b)
    product = mine + lax.ppermute(other, "core", [(0, 1), (1, 0)])

    axes = ("zlo", "x", "layer")
    blocks = product.reshape(lax.axis_size(axes), -1, columns)
    return lax.all_to_all(blocks, axes, 0, 0).sum(0)


def solution(mesh):
    rows, levels, layers = mesh.devices.shape
    shape = (rows // 2, 2, levels // 2, 2, layers)
    fine = Mesh(mesh.devices.reshape(shape), ("x", "core", "zhi", "zlo", "layer"))
    split_rows = ("x", "core", "layer")
    return jax.shard_map(
        on_device,
        mesh=fine,
        in_specs=(P(COL, split_rows), P(COL, split_rows)),
        out_specs=P(split_rows, COL),
        check_vma=False,
    )
```

```python
import jax
import jax.numpy as jnp
from jax import lax
from jax.experimental import pallas as pl
from jax.experimental.pallas import tpu as pltpu
from jax.sharding import Mesh
from jax.sharding import PartitionSpec as P

LEVELS = 8
EARLY = 48
COL = ("zhi", "zlo")
VMEM = pl.BlockSpec(memory_space=pltpu.VMEM)
SWAP_1 = [(i, i ^ 1) for i in range(LEVELS)]
SWAP_2 = [((i + 1) % LEVELS, (j + 1) % LEVELS) for i, j in SWAP_1]


def swap_1(array):
    return lax.ppermute(array, COL, SWAP_1)


def swap_2(array):
    return lax.ppermute(array, COL, SWAP_2)


def after(done, *payloads):
    return lax.optimization_barrier((*payloads, *done))[: len(payloads)]


def dot(left, right):
    return 0.5 * jnp.dot(
        left, right, precision=lax.Precision.HIGHEST, preferred_element_type=jnp.float32
    )


def transposed(array):
    def kernel(src, out):
        out[...] = src[...].T

    return pl.pallas_call(
        kernel,
        out_shape=jax.ShapeDtypeStruct(array.shape[::-1], array.dtype),
        in_specs=[VMEM],
        out_specs=VMEM,
        compiler_params=pltpu.CompilerParams(vmem_limit_bytes=16 * 1024 * 1024),
    )(array)


def row_level(level, distance):
    away = jnp.where(lax.rem(level, 2) == 0, distance % LEVELS, -distance % LEVELS)
    return lax.rem(level + away, LEVELS)


def multiply(blocks, distances, b, before):
    count = len(blocks)

    def kernel(*refs):
        b_ref, old, out = refs[count:]
        level = lax.axis_index("zhi") * 2 + lax.axis_index("zlo")
        out[...] = old[...]
        for ref, distance in zip(refs, distances):
            source = row_level(level, distance)
            out[lax.rem(source, 2), lax.axis_index("zlo"), source // 2] = dot(ref[...], b_ref[...])

    return pl.pallas_call(
        kernel,
        out_shape=jax.ShapeDtypeStruct(before.shape, jnp.float32),
        in_specs=[VMEM] * (count + 2),
        out_specs=VMEM,
        input_output_aliases={count + 1: 0},
        compiler_params=pltpu.CompilerParams(vmem_limit_bytes=24 * 1024 * 1024),
    )(*blocks, b, before)


def split(array):
    high = array.astype(jnp.bfloat16)
    return high, (array - high.astype(jnp.float32)).astype(jnp.bfloat16)


def split_stack(blocks):
    count, (rows, width) = len(blocks), blocks[0].shape

    def kernel(*refs):
        high, low = refs[count:]
        for i, ref in enumerate(refs[:count]):
            place = slice(i * rows, (i + 1) * rows)
            high[place, :], low[place, :] = split(ref[...])

    return pl.pallas_call(
        kernel,
        out_shape=[jax.ShapeDtypeStruct((count * rows, width), jnp.bfloat16)] * 2,
        in_specs=[VMEM] * count,
        out_specs=[VMEM] * 2,
        compiler_params=pltpu.CompilerParams(vmem_limit_bytes=24 * 1024 * 1024),
    )(*blocks)


def multiply_pair(stack, distances, b, pair_b, before):
    rows = before.shape[-2]

    def kernel(high, low, b_ref, *refs):
        pair_refs, old, out, both = refs[:-3], refs[-3], refs[-2], refs[-1]
        odd = lax.axis_index("zlo")
        level = lax.axis_index("zhi") * 2 + odd
        right = jnp.concatenate([ref[...] for ref in pair_refs], axis=0).T
        both[...] = jnp.concatenate([b_ref[...], right], axis=1)
        terms = jnp.concatenate(split(right), axis=1)
        width = right.shape[1]
        product = jnp.dot(high[...], terms, preferred_element_type=jnp.float32)
        product = product[:, :width] + (
            product[:, width:]
            + jnp.dot(low[...], terms[:, :width], preferred_element_type=jnp.float32)
        )
        out[...] = old[...]
        for i, distance in enumerate(distances):
            source = row_level(level, distance)
            block = product[i * rows : (i + 1) * rows]
            out[lax.rem(source, 2), 1 - odd, source // 2] = 0.5 * block

    return pl.pallas_call(
        kernel,
        out_shape=[
            jax.ShapeDtypeStruct(before.shape, jnp.float32),
            jax.ShapeDtypeStruct((b.shape[0], 2 * b.shape[1]), jnp.float32),
        ],
        in_specs=[VMEM] * (4 + len(pair_b)),
        out_specs=[VMEM] * 2,
        input_output_aliases={3 + len(pair_b): 0},
        compiler_params=pltpu.CompilerParams(vmem_limit_bytes=24 * 1024 * 1024),
    )(*stack, b, *pair_b, before)


def finish(last, both, before):
    def kernel(last_ref, both_ref, old, mine, other):
        core, odd = lax.axis_index("core"), lax.axis_index("zlo")
        level = lax.axis_index("zhi") * 2 + odd
        mine[...] = old[core]
        other[...] = old[1 - core]
        product = dot(last_ref[...], both_ref[...])
        width = product.shape[1] // 2
        source = row_level(level, LEVELS // 2)

        def store(out):
            out[odd, source // 2] = product[:, :width]
            out[1 - odd, source // 2] = product[:, width:]

        @pl.when(lax.rem(source, 2) == core)
        def _():
            store(mine)

        @pl.when(lax.rem(source, 2) != core)
        def _():
            store(other)

    return pl.pallas_call(
        kernel,
        out_shape=[jax.ShapeDtypeStruct(before.shape[1:], jnp.float32)] * 2,
        in_specs=[VMEM] * 3,
        out_specs=[VMEM] * 2,
        compiler_params=pltpu.CompilerParams(vmem_limit_bytes=24 * 1024 * 1024),
    )(last, both, before)


def on_device(amplitudes, integrals):
    level = lax.axis_index("zhi") * 2 + lax.axis_index("zlo")
    held = (level + 1) // 2 % 2
    rows, columns = amplitudes.shape[0], integrals.shape[0]
    half = amplitudes.shape[1] // 2

    def halves(array):
        low, high = array[:, :half], array[:, half:]
        return jnp.where(held == 0, low, high), jnp.where(held == 0, high, low)

    a_own, a_other = lax.optimization_barrier(halves(amplitudes))
    b_own, b_other = halves(integrals)

    far_1, far_2 = swap_1(a_own), swap_2(a_other)
    a_1, a_2 = swap_1(a_other), swap_2(a_own)
    a_3, far_3 = swap_1(far_2), swap_2(far_1)
    pair_early = swap_1(b_other[:EARLY])
    (a_1_on,) = after((a_2,), a_1)
    (far_3,) = after((pair_early,), far_3)
    a_4 = swap_2(a_1_on)
    a_5, a_6 = swap_1(far_3), swap_2(a_3)
    (b_late,) = after((a_4,), b_other[EARLY:])
    a_7, pair_late = swap_2(a_5), swap_1(b_late)

    b = transposed(b_own)
    product = jnp.zeros((2, 2, LEVELS // 2, rows, columns), jnp.float32)
    early, distances = [a_own, a_1, a_2, a_3, a_4, a_6, a_5], [0, 1, -1, 2, -2, -3, 3]
    for part in (slice(0, 3), slice(3, 5), slice(5, 7)):
        product = multiply(early[part], distances[part], b, product)
    pair_b = [pair_early, pair_late]
    product, both = multiply_pair(split_stack(early), distances, b, pair_b, product)
    mine, other = finish(a_7, both, product)
    product = mine + lax.ppermute(other, "core", [(0, 1), (1, 0)])

    axes = ("zlo", "x", "layer")
    blocks = product.reshape(lax.axis_size(axes), -1, columns)
    return lax.all_to_all(blocks, axes, 0, 0).sum(0)


def solution(mesh):
    rows, levels, layers = mesh.devices.shape
    shape = (rows // 2, 2, levels // 2, 2, layers)
    fine = Mesh(mesh.devices.reshape(shape), ("x", "core", "zhi", "zlo", "layer"))
    split_rows = ("x", "core", "layer")
    return jax.shard_map(
        on_device,
        mesh=fine,
        in_specs=(P(COL, split_rows), P(COL, split_rows)),
        out_specs=P(split_rows, COL),
        check_vma=False,
    )
```

```python
import jax
import jax.numpy as jnp
from jax import lax
from jax.experimental import pallas as pl
from jax.experimental.pallas import tpu as pltpu
from jax.sharding import Mesh
from jax.sharding import PartitionSpec as P

LEVELS = 8
EARLY = 48
COL = ("zhi", "zlo")
VMEM = pl.BlockSpec(memory_space=pltpu.VMEM)
SWAP_1 = [(i, i ^ 1) for i in range(LEVELS)]
SWAP_2 = [((i + 1) % LEVELS, (j + 1) % LEVELS) for i, j in SWAP_1]


def swap_1(array):
    return lax.ppermute(array, COL, SWAP_1)


def swap_2(array):
    return lax.ppermute(array, COL, SWAP_2)


def after(done, *payloads):
    return lax.optimization_barrier((*payloads, *done))[: len(payloads)]


def dot(left, right):
    return 0.5 * jnp.dot(
        left, right, precision=lax.Precision.HIGHEST, preferred_element_type=jnp.float32
    )


def transposed(array):
    def kernel(src, out):
        out[...] = src[...].T

    return pl.pallas_call(
        kernel,
        out_shape=jax.ShapeDtypeStruct(array.shape[::-1], array.dtype),
        in_specs=[VMEM],
        out_specs=VMEM,
        compiler_params=pltpu.CompilerParams(vmem_limit_bytes=16 * 1024 * 1024),
    )(array)


def row_level(level, distance):
    away = jnp.where(lax.rem(level, 2) == 0, distance % LEVELS, -distance % LEVELS)
    return lax.rem(level + away, LEVELS)


def multiply(blocks, distances, b, before):
    count = len(blocks)

    def kernel(*refs):
        b_ref, old, out = refs[count:]
        level = lax.axis_index("zhi") * 2 + lax.axis_index("zlo")
        out[...] = old[...]
        for ref, distance in zip(refs, distances):
            source = row_level(level, distance)
            out[lax.rem(source, 2), lax.axis_index("zlo"), source // 2] = dot(ref[...], b_ref[...])

    return pl.pallas_call(
        kernel,
        out_shape=jax.ShapeDtypeStruct(before.shape, jnp.float32),
        in_specs=[VMEM] * (count + 2),
        out_specs=VMEM,
        input_output_aliases={count + 1: 0},
        compiler_params=pltpu.CompilerParams(vmem_limit_bytes=24 * 1024 * 1024),
    )(*blocks, b, before)


def multiply_pair(blocks, distances, b, pair_b, before):
    count, rows = len(blocks), before.shape[-2]

    def kernel(*refs):
        b_ref, pair_refs = refs[count], refs[count + 1 : -3]
        old, out, both = refs[-3:]
        odd = lax.axis_index("zlo")
        level = lax.axis_index("zhi") * 2 + odd
        right = jnp.concatenate([ref[...] for ref in pair_refs], axis=0).T
        both[...] = jnp.concatenate([b_ref[...], right], axis=1)
        product = dot(jnp.concatenate([ref[...] for ref in refs[:count]], axis=0), right)
        out[...] = old[...]
        for i, distance in enumerate(distances):
            source = row_level(level, distance)
            block = product[i * rows : (i + 1) * rows]
            out[lax.rem(source, 2), 1 - odd, source // 2] = block

    n_in = count + 1 + len(pair_b)
    return pl.pallas_call(
        kernel,
        out_shape=[
            jax.ShapeDtypeStruct(before.shape, jnp.float32),
            jax.ShapeDtypeStruct((b.shape[0], 2 * b.shape[1]), jnp.float32),
        ],
        in_specs=[VMEM] * (n_in + 1),
        out_specs=[VMEM] * 2,
        input_output_aliases={n_in: 0},
        compiler_params=pltpu.CompilerParams(vmem_limit_bytes=32 * 1024 * 1024),
    )(*blocks, b, *pair_b, before)


def finish(last, both, before):
    def kernel(last_ref, both_ref, old, mine, other):
        core, odd = lax.axis_index("core"), lax.axis_index("zlo")
        level = lax.axis_index("zhi") * 2 + odd
        mine[...] = old[core]
        other[...] = old[1 - core]
        product = dot(last_ref[...], both_ref[...])
        width = product.shape[1] // 2
        source = row_level(level, LEVELS // 2)

        def store(out):
            out[odd, source // 2] = product[:, :width]
            out[1 - odd, source // 2] = product[:, width:]

        @pl.when(lax.rem(source, 2) == core)
        def _():
            store(mine)

        @pl.when(lax.rem(source, 2) != core)
        def _():
            store(other)

    return pl.pallas_call(
        kernel,
        out_shape=[jax.ShapeDtypeStruct(before.shape[1:], jnp.float32)] * 2,
        in_specs=[VMEM] * 3,
        out_specs=[VMEM] * 2,
        compiler_params=pltpu.CompilerParams(vmem_limit_bytes=24 * 1024 * 1024),
    )(last, both, before)


def on_device(amplitudes, integrals):
    level = lax.axis_index("zhi") * 2 + lax.axis_index("zlo")
    held = (level + 1) // 2 % 2
    rows, columns = amplitudes.shape[0], integrals.shape[0]
    half = amplitudes.shape[1] // 2

    def halves(array):
        low, high = array[:, :half], array[:, half:]
        return jnp.where(held == 0, low, high), jnp.where(held == 0, high, low)

    a_own, a_other = lax.optimization_barrier(halves(amplitudes))
    b_own, b_other = halves(integrals)

    far_1, far_2 = swap_1(a_own), swap_2(a_other)
    a_1, a_2 = swap_1(a_other), swap_2(a_own)
    a_3, far_3 = swap_1(far_2), swap_2(far_1)
    pair_early = swap_1(b_other[:EARLY])
    (a_1_on,) = after((a_2,), a_1)
    (far_3,) = after((pair_early,), far_3)
    a_4 = swap_2(a_1_on)
    a_5, a_6 = swap_1(far_3), swap_2(a_3)
    (b_late,) = after((a_4,), b_other[EARLY:])
    a_7, pair_late = swap_2(a_5), swap_1(b_late)

    b = transposed(b_own)
    product = jnp.zeros((2, 2, LEVELS // 2, rows, columns), jnp.float32)
    early, distances = [a_own, a_1, a_2, a_3, a_4, a_6, a_5], [0, 1, -1, 2, -2, -3, 3]
    for part in (slice(0, 3), slice(3, 5), slice(5, 7)):
        product = multiply(early[part], distances[part], b, product)
    pair_b = [pair_early, pair_late]
    product, both = multiply_pair(early, distances, b, pair_b, product)
    mine, other = finish(a_7, both, product)
    product = mine + lax.ppermute(other, "core", [(0, 1), (1, 0)])

    axes = ("zlo", "x", "layer")
    blocks = product.reshape(lax.axis_size(axes), -1, columns)
    return lax.all_to_all(blocks, axes, 0, 0).sum(0)


def solution(mesh):
    rows, levels, layers = mesh.devices.shape
    shape = (rows // 2, 2, levels // 2, 2, layers)
    fine = Mesh(mesh.devices.reshape(shape), ("x", "core", "zhi", "zlo", "layer"))
    split_rows = ("x", "core", "layer")
    return jax.shard_map(
        on_device,
        mesh=fine,
        in_specs=(P(COL, split_rows), P(COL, split_rows)),
        out_specs=P(split_rows, COL),
        check_vma=False,
    )
```

```python
import jax
import jax.numpy as jnp
from jax import lax
from jax.experimental import pallas as pl
from jax.experimental.pallas import tpu as pltpu
from jax.sharding import Mesh
from jax.sharding import PartitionSpec as P

LEVELS = 8
EARLY = 40
COL = ("zhi", "zlo")
VMEM = pl.BlockSpec(memory_space=pltpu.VMEM)
SWAP_1 = [(i, i ^ 1) for i in range(LEVELS)]
SWAP_2 = [((i + 1) % LEVELS, (j + 1) % LEVELS) for i, j in SWAP_1]


def swap_1(array):
    return lax.ppermute(array, COL, SWAP_1)


def swap_2(array):
    return lax.ppermute(array, COL, SWAP_2)


def after(done, *payloads):
    return lax.optimization_barrier((*payloads, *done))[: len(payloads)]


def dot(left, right):
    return 0.5 * jnp.dot(
        left, right, precision=lax.Precision.HIGHEST, preferred_element_type=jnp.float32
    )


def transposed(array):
    def kernel(src, out):
        out[...] = src[...].T

    return pl.pallas_call(
        kernel,
        out_shape=jax.ShapeDtypeStruct(array.shape[::-1], array.dtype),
        in_specs=[VMEM],
        out_specs=VMEM,
        compiler_params=pltpu.CompilerParams(vmem_limit_bytes=16 * 1024 * 1024),
    )(array)


def row_level(level, distance):
    away = jnp.where(lax.rem(level, 2) == 0, distance % LEVELS, -distance % LEVELS)
    return lax.rem(level + away, LEVELS)


def multiply(blocks, distances, b, before):
    count = len(blocks)

    def kernel(*refs):
        b_ref, old, out = refs[count:]
        level = lax.axis_index("zhi") * 2 + lax.axis_index("zlo")
        out[...] = old[...]
        for ref, distance in zip(refs, distances):
            source = row_level(level, distance)
            out[lax.rem(source, 2), lax.axis_index("zlo"), source // 2] = dot(ref[...], b_ref[...])

    return pl.pallas_call(
        kernel,
        out_shape=jax.ShapeDtypeStruct(before.shape, jnp.float32),
        in_specs=[VMEM] * (count + 2),
        out_specs=VMEM,
        input_output_aliases={count + 1: 0},
        compiler_params=pltpu.CompilerParams(vmem_limit_bytes=24 * 1024 * 1024),
    )(*blocks, b, before)


def multiply_pair(blocks, distances, b, pair_b, before):
    count, rows = len(blocks), before.shape[-2]

    def kernel(*refs):
        b_ref, pair_refs = refs[count], refs[count + 1 : -3]
        old, out, both = refs[-3:]
        odd = lax.axis_index("zlo")
        level = lax.axis_index("zhi") * 2 + odd
        right = jnp.concatenate([ref[...] for ref in pair_refs], axis=0).T
        both[...] = jnp.concatenate([b_ref[...], right], axis=1)
        product = dot(jnp.concatenate([ref[...] for ref in refs[:count]], axis=0), right)
        out[...] = old[...]
        for i, distance in enumerate(distances):
            source = row_level(level, distance)
            block = product[i * rows : (i + 1) * rows]
            out[lax.rem(source, 2), 1 - odd, source // 2] = block

    n_in = count + 1 + len(pair_b)
    return pl.pallas_call(
        kernel,
        out_shape=[
            jax.ShapeDtypeStruct(before.shape, jnp.float32),
            jax.ShapeDtypeStruct((b.shape[0], 2 * b.shape[1]), jnp.float32),
        ],
        in_specs=[VMEM] * (n_in + 1),
        out_specs=[VMEM] * 2,
        input_output_aliases={n_in: 0},
        compiler_params=pltpu.CompilerParams(vmem_limit_bytes=32 * 1024 * 1024),
    )(*blocks, b, *pair_b, before)


def finish(last, both, before):
    def kernel(last_ref, both_ref, old, mine, other):
        core, odd = lax.axis_index("core"), lax.axis_index("zlo")
        level = lax.axis_index("zhi") * 2 + odd
        mine[...] = old[core]
        other[...] = old[1 - core]
        product = dot(last_ref[...], both_ref[...])
        width = product.shape[1] // 2
        source = row_level(level, LEVELS // 2)

        def store(out):
            out[odd, source // 2] = product[:, :width]
            out[1 - odd, source // 2] = product[:, width:]

        @pl.when(lax.rem(source, 2) == core)
        def _():
            store(mine)

        @pl.when(lax.rem(source, 2) != core)
        def _():
            store(other)

    return pl.pallas_call(
        kernel,
        out_shape=[jax.ShapeDtypeStruct(before.shape[1:], jnp.float32)] * 2,
        in_specs=[VMEM] * 3,
        out_specs=[VMEM] * 2,
        compiler_params=pltpu.CompilerParams(vmem_limit_bytes=24 * 1024 * 1024),
    )(last, both, before)


def on_device(amplitudes, integrals):
    level = lax.axis_index("zhi") * 2 + lax.axis_index("zlo")
    held = (level + 1) // 2 % 2
    rows, columns = amplitudes.shape[0], integrals.shape[0]
    half = amplitudes.shape[1] // 2

    def halves(array):
        low, high = array[:, :half], array[:, half:]
        return jnp.where(held == 0, low, high), jnp.where(held == 0, high, low)

    a_own, a_other = lax.optimization_barrier(halves(amplitudes))
    b_own, b_other = halves(integrals)

    far_1, far_2 = swap_1(a_own), swap_2(a_other)
    a_1, a_2 = swap_1(a_other), swap_2(a_own)
    a_3, far_3 = swap_1(far_2), swap_2(far_1)
    pair_early = swap_1(b_other[:EARLY])
    (a_1_on,) = after((a_2,), a_1)
    (far_3,) = after((pair_early,), far_3)
    a_4 = swap_2(a_1_on)
    a_5, a_6 = swap_1(far_3), swap_2(a_3)
    (b_late,) = after((a_4,), b_other[EARLY:])
    a_7, pair_late = swap_2(a_5), swap_1(b_late)

    b = transposed(b_own)
    product = jnp.zeros((2, 2, LEVELS // 2, rows, columns), jnp.float32)
    early, distances = [a_own, a_1, a_2, a_3, a_4, a_6, a_5], [0, 1, -1, 2, -2, -3, 3]
    for part in (slice(0, 3), slice(3, 5), slice(5, 7)):
        product = multiply(early[part], distances[part], b, product)
    pair_b = [pair_early, pair_late]
    product, both = multiply_pair(early, distances, b, pair_b, product)
    mine, other = finish(a_7, both, product)
    product = mine + lax.ppermute(other, "core", [(0, 1), (1, 0)])

    axes = ("zlo", "x", "layer")
    blocks = product.reshape(lax.axis_size(axes), -1, columns)
    return lax.all_to_all(blocks, axes, 0, 0).sum(0)


def solution(mesh):
    rows, levels, layers = mesh.devices.shape
    shape = (rows // 2, 2, levels // 2, 2, layers)
    fine = Mesh(mesh.devices.reshape(shape), ("x", "core", "zhi", "zlo", "layer"))
    split_rows = ("x", "core", "layer")
    return jax.shard_map(
        on_device,
        mesh=fine,
        in_specs=(P(COL, split_rows), P(COL, split_rows)),
        out_specs=P(split_rows, COL),
        check_vma=False,
    )
```

```python
import jax
import jax.numpy as jnp
from jax import lax
from jax.experimental import pallas as pl
from jax.experimental.pallas import tpu as pltpu
from jax.sharding import Mesh
from jax.sharding import PartitionSpec as P

LEVELS = 8
EARLY = 48
COL = ("zhi", "zlo")
VMEM = pl.BlockSpec(memory_space=pltpu.VMEM)
SWAP_1 = [(i, i ^ 1) for i in range(LEVELS)]
SWAP_2 = [((i + 1) % LEVELS, (j + 1) % LEVELS) for i, j in SWAP_1]


def swap_1(array):
    return lax.ppermute(array, COL, SWAP_1)


def swap_2(array):
    return lax.ppermute(array, COL, SWAP_2)


def after(done, *payloads):
    return lax.optimization_barrier((*payloads, *done))[: len(payloads)]


def dot(left, right):
    return 0.5 * jnp.dot(
        left, right, precision=lax.Precision.HIGHEST, preferred_element_type=jnp.float32
    )


def transposed(array):
    def kernel(src, out):
        out[...] = src[...].T

    return pl.pallas_call(
        kernel,
        out_shape=jax.ShapeDtypeStruct(array.shape[::-1], array.dtype),
        in_specs=[VMEM],
        out_specs=VMEM,
        compiler_params=pltpu.CompilerParams(vmem_limit_bytes=16 * 1024 * 1024),
    )(array)


def row_level(level, distance):
    away = jnp.where(lax.rem(level, 2) == 0, distance % LEVELS, -distance % LEVELS)
    return lax.rem(level + away, LEVELS)


def multiply(blocks, distances, b, before):
    count = len(blocks)

    def kernel(*refs):
        b_ref, old, out = refs[count:]
        level = lax.axis_index("zhi") * 2 + lax.axis_index("zlo")
        out[...] = old[...]
        for ref, distance in zip(refs, distances):
            source = row_level(level, distance)
            out[lax.rem(source, 2), lax.axis_index("zlo"), source // 2] = dot(ref[...], b_ref[...])

    return pl.pallas_call(
        kernel,
        out_shape=jax.ShapeDtypeStruct(before.shape, jnp.float32),
        in_specs=[VMEM] * (count + 2),
        out_specs=VMEM,
        input_output_aliases={count + 1: 0},
        compiler_params=pltpu.CompilerParams(vmem_limit_bytes=24 * 1024 * 1024),
    )(*blocks, b, before)


def multiply_pair(blocks, distances, b, pair_b, before):
    count, rows = len(blocks), before.shape[-2]

    def kernel(*refs):
        b_ref, pair_refs = refs[count], refs[count + 1 : -3]
        old, out, both = refs[-3:]
        odd = lax.axis_index("zlo")
        level = lax.axis_index("zhi") * 2 + odd
        right = jnp.concatenate([ref[...] for ref in pair_refs], axis=0).T
        both[...] = jnp.concatenate([b_ref[...], right], axis=1)
        product = dot(jnp.concatenate([ref[...] for ref in refs[:count]], axis=0), right)
        out[...] = old[...]
        for i, distance in enumerate(distances):
            source = row_level(level, distance)
            block = product[i * rows : (i + 1) * rows]
            out[lax.rem(source, 2), 1 - odd, source // 2] = block

    n_in = count + 1 + len(pair_b)
    return pl.pallas_call(
        kernel,
        out_shape=[
            jax.ShapeDtypeStruct(before.shape, jnp.float32),
            jax.ShapeDtypeStruct((b.shape[0], 2 * b.shape[1]), jnp.float32),
        ],
        in_specs=[VMEM] * (n_in + 1),
        out_specs=[VMEM] * 2,
        input_output_aliases={n_in: 0},
        compiler_params=pltpu.CompilerParams(vmem_limit_bytes=32 * 1024 * 1024),
    )(*blocks, b, *pair_b, before)


def finish(last, both, before):
    def kernel(last_ref, both_ref, old, mine, other):
        core, odd = lax.axis_index("core"), lax.axis_index("zlo")
        level = lax.axis_index("zhi") * 2 + odd
        mine[...] = old[core]
        other[...] = old[1 - core]
        product = dot(last_ref[...], both_ref[...])
        width = product.shape[1] // 2
        source = row_level(level, LEVELS // 2)

        def store(out):
            out[odd, source // 2] = product[:, :width]
            out[1 - odd, source // 2] = product[:, width:]

        @pl.when(lax.rem(source, 2) == core)
        def _():
            store(mine)

        @pl.when(lax.rem(source, 2) != core)
        def _():
            store(other)

    return pl.pallas_call(
        kernel,
        out_shape=[jax.ShapeDtypeStruct(before.shape[1:], jnp.float32)] * 2,
        in_specs=[VMEM] * 3,
        out_specs=[VMEM] * 2,
        compiler_params=pltpu.CompilerParams(vmem_limit_bytes=24 * 1024 * 1024),
    )(last, both, before)


def on_device(amplitudes, integrals):
    level = lax.axis_index("zhi") * 2 + lax.axis_index("zlo")
    held = (level + 1) // 2 % 2
    rows, columns = amplitudes.shape[0], integrals.shape[0]
    half = amplitudes.shape[1] // 2

    def halves(array):
        low, high = array[:, :half], array[:, half:]
        return jnp.where(held == 0, low, high), jnp.where(held == 0, high, low)

    a_own, a_other = halves(amplitudes)
    b_own, b_other = halves(integrals)

    far_1, far_2 = swap_1(a_own), swap_2(a_other)
    a_1, a_2 = swap_1(a_other), swap_2(a_own)
    a_3, far_3 = swap_1(far_2), swap_2(far_1)
    pair_early = swap_1(b_other[:EARLY])
    (a_1_on,) = after((a_2,), a_1)
    (far_3,) = after((pair_early,), far_3)
    a_4 = swap_2(a_1_on)
    a_5, a_6 = swap_1(far_3), swap_2(a_3)
    (b_late,) = after((a_4,), b_other[EARLY:])
    a_7, pair_late = swap_2(a_5), swap_1(b_late)

    b = transposed(b_own)
    product = jnp.zeros((2, 2, LEVELS // 2, rows, columns), jnp.float32)
    early, distances = [a_own, a_1, a_2, a_3, a_4, a_6, a_5], [0, 1, -1, 2, -2, -3, 3]
    for part in (slice(0, 3), slice(3, 5), slice(5, 7)):
        product = multiply(early[part], distances[part], b, product)
    pair_b = [pair_early, pair_late]
    product, both = multiply_pair(early, distances, b, pair_b, product)
    mine, other = finish(a_7, both, product)
    product = mine + lax.ppermute(other, "core", [(0, 1), (1, 0)])

    axes = ("zlo", "x", "layer")
    blocks = product.reshape(lax.axis_size(axes), -1, columns)
    return lax.all_to_all(blocks, axes, 0, 0).sum(0)


def solution(mesh):
    rows, levels, layers = mesh.devices.shape
    shape = (rows // 2, 2, levels // 2, 2, layers)
    fine = Mesh(mesh.devices.reshape(shape), ("x", "core", "zhi", "zlo", "layer"))
    split_rows = ("x", "core", "layer")
    return jax.shard_map(
        on_device,
        mesh=fine,
        in_specs=(P(COL, split_rows), P(COL, split_rows)),
        out_specs=P(split_rows, COL),
        check_vma=False,
    )
```
